32 devices in a mesh: groups: 2 (over y), row: 2 (over core), col: 8 (over z, x).
Axes of the slice: x: 2, y: 2, z: 4, core: 2. Of those that a mesh axis runs over, the one named last changes fastest.
Arguments:
- block_values: float32 [160, 2, 64, 640], P(('groups', 'col'), 'row'), parts along dimension 0, may hold values from -1.2 to 1.2
- block_cols: int32 [160, 2, 10], P(('groups', 'col'), 'row'), parts along dimension 0, may hold values from -1 to 79, as said below
Outputs:
- block_product: float32 [160, 2, 64, 640], P(('groups', 'col'), 'row'), parts along dimension 0
The draws below stay inside these ranges and needn't reach their ends.
There are 2 independent parts, one for each index of `groups`. The reference program is written for one: setup_inputs(seed, part) draws one part's arguments, and reference() takes and returns one part's arrays. A program takes and returns all parts, laid end to end along the dimension named above; each array names one. Nothing has to cross between parts.
Inputs may be any that keep to these rules, and one draw needn't show every extreme that they name: Each live entry of block_cols[i, p, :] is a block column j with j % 2 == p and |j - i| <= 10; the live entries of one list are distinct and stand before its -1 entries; every list holds at least one live entry; some list holds 10; how many are live varies from band to band.
All inputs are finite; a program needn't handle non-finite values.
Results may differ from the reference program's by a relative error of at most 0.0003.
Values sent between devices are 32-bit elements; how exact they have to be, the bound alone decides.
A program may use at most 128 MiB of HBM per device.

```python
import jax
import jax.numpy as jnp
from jax import lax

BS = 64
K = 10
REACH = 10
BAND = 10
NB = 80


def draw_block_cols(key, part):
    key = jax.random.fold_in(key, 11)
    key_score, key_low, key_count, key_full = jax.random.split(key, 4)
    span = 2 * REACH + 1
    row_ids = jnp.arange(NB, dtype=jnp.int32)[:, None, None]
    parity = jnp.arange(2, dtype=jnp.int32)[None, :, None]
    offsets = jnp.arange(span, dtype=jnp.int32)[None, None, :] - REACH
    candidate = row_ids + offsets
    usable = (candidate >= 0) & (candidate < NB) & (candidate % 2 == parity)
    scores = jax.random.randint(key_score, (NB, 2, span), 0, 1 << 20) * 64 + jnp.arange(span, dtype=jnp.int32)[None, None, :]
    scores = jnp.where(usable, scores, 1 << 30)
    ranking = jnp.argsort(scores, axis=-1, stable=True)[..., :K]
    chosen = jnp.take_along_axis(candidate, ranking, axis=-1)
    available = jnp.sum(usable.astype(jnp.int32), axis=-1)
    band_low = jax.random.randint(key_low, (NB // BAND,), 1, K + 1)
    row_low = jnp.repeat(band_low, BAND)[:, None]
    drawn = jax.random.randint(key_count, (NB, 2), 0, 1 << 20)
    counts = drawn % (K + 1 - row_low) + row_low
    full_pick = jax.random.randint(key_full, (NB // BAND,), 0, BAND)
    in_band = jnp.arange(NB, dtype=jnp.int32) % BAND
    forced = in_band == jnp.repeat(full_pick, BAND)
    counts = jnp.where(forced[:, None], K, counts)
    counts = jnp.minimum(counts, available)
    slot_ids = jnp.arange(K, dtype=jnp.int32)[None, None, :]
    return jnp.where(slot_ids < counts[:, :, None], chosen, -1).astype(jnp.int32)


def level_of(key, dims, cuts, least, high):
    factor_of = 1.0
    for position, shards_of in cuts:
        draws = jax.random.uniform(jax.random.fold_in(jax.random.fold_in(key, 6), position), (shards_of,), jnp.float32, least / len(cuts), high / len(cuts))
        factor_of = factor_of * jnp.repeat(jnp.exp(draws), dims[position] // shards_of).reshape((-1,) + (1,) * (len(dims) - 1 - position))
    return factor_of


def noise(stream_key, extent, deviation, reach, cuts=(), kind=jnp.bfloat16):
    values = jax.random.normal(stream_key, extent, jnp.float32) * deviation
    if len(cuts) > 0:
        values = level_of(stream_key, extent, cuts, -0.22, 0.18) * values
    return jnp.clip(values, min=-reach, max=reach).astype(kind)


def setup_inputs(seed: int = 0, part: int = 0) -> dict:
    arg_keys = jax.random.split(jax.random.key(seed), 3)
    part_keys = jax.random.split(jax.random.fold_in(arg_keys[2], part), 3)
    return {
        "block_values": noise(part_keys[0], (NB, 2, BS, K * BS), 0.2, 1.2, ((0, 8), (1, 2)), jnp.float32),
        "block_cols": draw_block_cols(jax.random.fold_in(jax.random.fold_in(arg_keys[2], part), 71), part),
    }


def reference(block_values, block_cols):
    live_slot = block_cols >= 0
    blocks = block_values.reshape(NB, 2, BS, K, BS)
    blocks = jnp.where(live_slot[:, :, None, :, None], blocks, 0.0)

    def one_row(row_index):
        row_cols = block_cols[row_index]
        left_blocks = blocks[row_index].transpose(0, 2, 1, 3).reshape(2 * K, BS, BS)
        inner = jnp.maximum(row_cols.reshape(2 * K), 0).astype(jnp.int32)
        right_blocks = jnp.take(blocks, inner, axis=0)
        right_cols = jnp.take(block_cols, inner, axis=0)
        matches = (right_cols[:, :, :, None] == row_cols[None, :, None, :]) & (right_cols[:, :, :, None] >= 0) & (row_cols[None, :, None, :] >= 0)
        mapped = jnp.einsum("qpbud,qpus->qpbsd", right_blocks, matches.astype(jnp.float32), precision=lax.Precision.HIGHEST)
        product = jnp.einsum("qab,qpbsd->pasd", left_blocks, mapped, precision=lax.Precision.HIGHEST)
        return product.reshape(2, BS, K * BS)

    return lax.map(one_row, jnp.arange(NB, dtype=jnp.int32))
```

```python
import functools

import jax
import jax.numpy as jnp
from jax import lax
from jax.experimental import pallas as pl
from jax.experimental.pallas import tpu as pltpu
from jax.sharding import PartitionSpec as P

REACH = 10
CHUNK = 2
OWN_AT, X_AT, F_AT, OUT_AT = 0, 32, 64, 96
MESH = pl.DeviceIdType.MESH


def picked(codes, tiles):
    high = (lax.broadcasted_iota(jnp.int32, (8, 128), 1) >= 64).astype(jnp.int32)
    kept, turned = codes - high, codes + high
    x = jnp.zeros((8, 8, 128), jnp.float32)
    for u, (plain, rolled) in enumerate(tiles):
        x = jnp.where((kept == 2 * u)[None], plain, x)
        x = jnp.where((turned == 2 * u + 1)[None], rolled, x)
    return x


def rolled(x):
    return pltpu.roll(x.reshape(64, 128), 64, 1).reshape(8, 8, 128)


def low_half(shape):
    return lax.broadcasted_iota(jnp.int32, shape, len(shape) - 1) < 64


def pair(low, low_at, high, high_at):
    first = jnp.broadcast_to(low[:, low_at:low_at + 1], (8, 128))
    second = jnp.broadcast_to(high[:, high_at:high_at + 1], (8, 128))
    return jnp.where(low_half((8, 128)), first, second)


def split(x):
    x = x.reshape(64, 128)
    hi = x.astype(jnp.bfloat16)
    return hi, (x - hi.astype(jnp.float32)).astype(jnp.bfloat16)


def kernel(
    n_col, band, slots, vals, inv, out,
    both, x_buf, f_buf, stage, b_hi, b_lo, a_hi, a_lo, acc, inv_o, inv_x, inv_f,
    x_send, x_recv, f_send, f_recv, c_sem, t_send, t_recv, l_sem,
):
    g, p, c = lax.axis_index("groups"), lax.axis_index("row"), lax.axis_index("col")
    chunks = band // CHUNK
    tiles = acc.shape[0]
    k_tiles = a_hi.shape[0]
    odd = lax.rem(c, 2)
    x_peer = c + 1 - 2 * odd
    f_to, f_from = c + 2 - 4 * odd, c - 2 + 4 * odd
    has_to = (f_to >= 0) & (f_to < n_col)
    has_from = (f_from >= 0) & (f_from < n_col)
    core_id, x_id = (g, 1 - p, c), (g, p, x_peer)
    to_id = (g, p, jnp.clip(f_to, 0, n_col - 1))
    from_id = (g, p, jnp.clip(f_from, 0, n_col - 1))

    barrier = pltpu.get_barrier_semaphore()
    for peer in (core_id, x_id):
        pl.semaphore_signal(barrier, inc=1, device_id=peer, device_id_type=MESH)

    @pl.when(has_to)
    def _():
        pl.semaphore_signal(barrier, inc=1, device_id=to_id, device_id_type=MESH)

    @pl.when(has_from)
    def _():
        pl.semaphore_signal(barrier, inc=1, device_id=from_id, device_id_type=MESH)

    pl.semaphore_wait(barrier, 2 + has_to.astype(jnp.int32) + has_from.astype(jnp.int32))

    def remote(src, dst, send, recv, device):
        return pltpu.make_async_remote_copy(
            src_ref=src, dst_ref=dst, send_sem=send, recv_sem=recv,
            device_id=device, device_id_type=MESH,
        )

    def rows(ch):
        return pl.ds(ch * CHUNK, CHUNK)

    def x_copy(ch):
        return remote(vals.at[rows(ch), 0], x_buf.at[rows(ch)], x_send.at[ch], x_recv.at[ch], x_id)

    def f_copy(ch):
        return remote(x_buf.at[rows(ch)], f_buf.at[rows(ch)], f_send.at[ch], f_recv.at[ch], to_id)

    tab_c = remote(inv, inv_o, t_send.at[0], t_recv.at[0], core_id)
    tab_x = remote(inv, inv_x, t_send.at[1], t_recv.at[1], x_id)
    tab_f = remote(inv_x, inv_f, t_send.at[2], t_recv.at[2], to_id)
    core = remote(vals.at[:, 0], both.at[p], c_sem.at[0], c_sem.at[1], core_id)
    own = pltpu.make_async_copy(vals.at[:, 0], both.at[p], l_sem)
    tab_x.start()
    tab_c.start()
    x_copy(0).start()
    core.start()
    own.start()
    for ch in range(1, chunks):
        x_copy(ch).start()

    acc[...] = jnp.zeros_like(acc)
    own.wait()
    core.wait()
    tab_c.wait()
    tab_x.wait()

    @pl.when(has_to)
    def _():
        tab_f.start()

    def a_row(i, carry):
        at = pl.ds(pl.multiple_of(i * 64, 64), 64)
        low = low_half((8, 8, 128))
        held = []
        for u in range(slots // 2):
            even = both[0, i, :, u * 128:(u + 1) * 128].reshape(8, 8, 128)
            odd = both[1, i, :, u * 128:(u + 1) * 128].reshape(8, 8, 128)
            held.append((jnp.where(low, even, odd), rolled(jnp.where(low, odd, even))))
        mine, other = inv[pl.ds(i, 1), :], inv_o[pl.ds(i, 1), :]
        first = jnp.where(p == 0, mine, other)
        second = jnp.where(p == 0, other, mine)
        for t in range(k_tiles):
            hi, lo = split(picked(pair(first, OWN_AT + t, second, OWN_AT + t), held))
            a_hi[t, at, :] = hi
            a_lo[t, at, :] = lo
        return carry

    lax.fori_loop(0, band, a_row, 0)

    def multiply(ch, table, first, k_tile):
        for r in range(CHUNK):
            codes = table[pl.ds(ch * CHUNK + r, 1), :]
            held = []
            for u in range(slots // 2):
                tile = stage[r, :, u * 128:(u + 1) * 128].reshape(8, 8, 128)
                held.append((tile, rolled(tile)))
            for t in range(tiles):
                at = first + 2 * t
                hi, lo = split(picked(pair(codes, at, codes, at + 1), held))
                b_hi[r * 64:(r + 1) * 64, t * 128:(t + 1) * 128] = hi
                b_lo[r * 64:(r + 1) * 64, t * 128:(t + 1) * 128] = lo
        left_hi = a_hi[k_tile]
        left = jnp.concatenate([left_hi, left_hi, a_lo[k_tile]], axis=1)
        for t in range(0, tiles, 2):
            at = slice(t * 128, (t + 2) * 128)
            right_hi = b_hi[:, at]
            right = jnp.concatenate([right_hi, b_lo[:, at], right_hi], axis=0)
            part = jnp.dot(left, right, preferred_element_type=jnp.float32)
            acc[t] += part[:, :128]
            acc[t + 1] += part[:, 128:]

    half = band // 2
    x_shift = half * (1 - 2 * odd)
    own_tile = REACH // 2
    x_tile = own_tile + x_shift
    f_tile = own_tile - x_shift

    def x_wait(ch):
        x_copy(ch).wait_recv()

        @pl.when(has_to)
        def _():
            f_copy(ch).start()

    def own_step(ch, carry):
        x_wait(ch)
        stage[...] = both[p, rows(ch)]
        multiply(ch, inv, OWN_AT, own_tile + ch)
        return carry

    lax.fori_loop(0, chunks, own_step, 0)

    def x_step(ch, carry):
        stage[...] = x_buf[rows(ch)]
        multiply(ch, inv_x, X_AT, x_tile + ch)
        return carry

    lax.fori_loop(0, chunks, x_step, 0)

    @pl.when(has_from)
    def _():
        tab_f.wait_recv()

        def f_step(ch, carry):
            f_copy(ch).wait_recv()
            stage[...] = f_buf[rows(ch)]
            multiply(ch, inv_f, F_AT, f_tile + ch)
            return carry

        lax.fori_loop(0, chunks, f_step, 0)

    def out_row(i, carry):
        at = pl.ds(pl.multiple_of(i * 64, 64), 64)
        held = []
        for u in range(tiles):
            tile = acc[u, at, :].reshape(8, 8, 128)
            held.append((tile, rolled(tile)))
        codes = inv[pl.ds(i, 1), :]
        for t in range(slots // 2):
            put = OUT_AT + 2 * t
            x = picked(pair(codes, put, codes, put + 1), held)
            out[i, 0, :, t * 128:(t + 1) * 128] = x.reshape(64, 128)
        return carry

    lax.fori_loop(0, band, out_row, 0)

    for ch in range(chunks):
        x_copy(ch).wait_send()

    @pl.when(has_to)
    def _():
        tab_f.wait_send()
        for ch in range(chunks):
            f_copy(ch).wait_send()


def local(n_col, block_values, block_cols):
    band, _, side, _ = block_values.shape
    cols = block_cols[:, 0]
    slots = cols.shape[1]
    col = lax.axis_index("col")
    base = col * band - REACH + lax.axis_index("row")
    shift = (band // 2) * (1 - 2 * lax.rem(col, 2))
    places = jnp.arange(32, dtype=jnp.int32)
    views = base + 2 * jnp.concatenate([places, places + shift, places - shift])
    found = (cols[:, :, None] == views[None, None, :]) & (cols >= 0)[:, :, None]
    inv = jnp.max(
        jnp.where(found, jnp.arange(slots, dtype=jnp.int32)[None, :, None], -1), axis=1
    )
    where_to = jnp.where(cols >= 0, (cols - base) >> 1, -1)
    rows = -(-band // 8) * 8
    inv = jnp.concatenate([inv, where_to], axis=1)
    inv = jnp.pad(inv, ((0, rows - band), (0, 128 - inv.shape[1])))
    k_tiles = (2 * REACH + band) // 2
    tiles = (k_tiles + 1) // 2
    chunks = band // CHUNK
    dma = pltpu.SemaphoreType.DMA
    return pl.pallas_call(
        functools.partial(kernel, n_col, band, slots),
        out_shape=jax.ShapeDtypeStruct(block_values.shape, jnp.float32),
        in_specs=[
            pl.BlockSpec(memory_space=pl.ANY),
            pl.BlockSpec(memory_space=pltpu.VMEM),
        ],
        out_specs=pl.BlockSpec(memory_space=pltpu.VMEM),
        scratch_shapes=[
            pltpu.VMEM((2, band, side, slots * side), jnp.float32),
            pltpu.VMEM((band, side, slots * side), jnp.float32),
            pltpu.VMEM((band, side, slots * side), jnp.float32),
            pltpu.VMEM((CHUNK, side, slots * side), jnp.float32),
            pltpu.VMEM((CHUNK * side, tiles * 128), jnp.bfloat16),
            pltpu.VMEM((CHUNK * side, tiles * 128), jnp.bfloat16),
            pltpu.VMEM((k_tiles, band * side, 128), jnp.bfloat16),
            pltpu.VMEM((k_tiles, band * side, 128), jnp.bfloat16),
            pltpu.VMEM((tiles, band * side, 128), jnp.float32),
            pltpu.VMEM((rows, 128), jnp.int32),
            pltpu.VMEM((rows, 128), jnp.int32),
            pltpu.VMEM((rows, 128), jnp.int32),
            dma((chunks,)), dma((chunks,)), dma((chunks,)), dma((chunks,)),
            dma((2,)), dma((3,)), dma((3,)), dma,
        ],
        compiler_params=pltpu.CompilerParams(
            collective_id=0, has_side_effects=True, vmem_limit_bytes=48 * 1024 * 1024
        ),
    )(block_values, inv)


def solution(mesh):
    in_specs = (P(("groups", "col"), "row", None, None), P(("groups", "col"), "row", None))
    out_specs = P(("groups", "col"), "row", None, None)
    return jax.shard_map(
        functools.partial(local, mesh.shape["col"]),
        mesh=mesh, in_specs=in_specs, out_specs=out_specs, check_vma=False,
    )
```

```python
import functools

import jax
import jax.numpy as jnp
from jax import lax
from jax.experimental import pallas as pl
from jax.experimental.pallas import tpu as pltpu
from jax.sharding import PartitionSpec as P

REACH = 10
CHUNK = 2
OWN_AT, X_AT, F_AT = 0, 32, 64
MESH = pl.DeviceIdType.MESH


def picked(codes, tiles):
    high = (lax.broadcasted_iota(jnp.int32, (8, 128), 1) >= 64).astype(jnp.int32)
    kept, turned = codes - high, codes + high
    x = jnp.zeros((8, 8, 128), jnp.float32)
    for u, (plain, rolled) in enumerate(tiles):
        x = jnp.where((kept == 2 * u)[None], plain, x)
        x = jnp.where((turned == 2 * u + 1)[None], rolled, x)
    return x


def rolled(x):
    return pltpu.roll(x.reshape(64, 128), 64, 1).reshape(8, 8, 128)


def low_half(shape):
    return lax.broadcasted_iota(jnp.int32, shape, len(shape) - 1) < 64


def pair(low, low_at, high, high_at):
    first = jnp.broadcast_to(low[:, low_at:low_at + 1], (8, 128))
    second = jnp.broadcast_to(high[:, high_at:high_at + 1], (8, 128))
    return jnp.where(low_half((8, 128)), first, second)


def split(x):
    x = x.reshape(64, 128)
    hi = x.astype(jnp.bfloat16)
    return hi, (x - hi.astype(jnp.float32)).astype(jnp.bfloat16)


def kernel(
    n_col, band, slots, vals, cols, out,
    both, x_buf, f_buf, stage, b_hi, b_lo, a_hi, a_lo, acc, cols_v, put_v, inv, inv_o, inv_x, inv_f,
    x_send, x_recv, f_send, f_recv, c_sem, t_send, t_recv, l_sem,
):
    g, p, c = lax.axis_index("groups"), lax.axis_index("row"), lax.axis_index("col")
    chunks = band // CHUNK
    tiles = acc.shape[0]
    k_tiles = a_hi.shape[0]
    half = band // 2
    odd = lax.rem(c, 2)
    x_peer = c + 1 - 2 * odd
    x_shift = half * (1 - 2 * odd)
    f_to, f_from = c + 2 - 4 * odd, c - 2 + 4 * odd
    has_to = (f_to >= 0) & (f_to < n_col)
    has_from = (f_from >= 0) & (f_from < n_col)
    core_id, x_id = (g, 1 - p, c), (g, p, x_peer)
    to_id = (g, p, jnp.clip(f_to, 0, n_col - 1))
    from_id = (g, p, jnp.clip(f_from, 0, n_col - 1))

    own = pltpu.make_async_copy(vals.at[:, 0], both.at[p], l_sem.at[0])
    lists = pltpu.make_async_copy(cols, cols_v, l_sem.at[1])
    lists.start()
    own.start()

    barrier = pltpu.get_barrier_semaphore()
    for peer in (core_id, x_id):
        pl.semaphore_signal(barrier, inc=1, device_id=peer, device_id_type=MESH)

    @pl.when(has_to)
    def _():
        pl.semaphore_signal(barrier, inc=1, device_id=to_id, device_id_type=MESH)

    @pl.when(has_from)
    def _():
        pl.semaphore_signal(barrier, inc=1, device_id=from_id, device_id_type=MESH)

    lists.wait()
    column = cols_v[:, 0, :]
    base = c * band - REACH + p
    lane = lax.broadcasted_iota(jnp.int32, (band, 128), 1)
    view = lane >> 5
    moved = jnp.where(view == 1, x_shift, jnp.where(view == 2, -x_shift, 0))
    wanted = base + 2 * ((lane & 31) + moved)
    codes = jnp.full((band, 128), -1, jnp.int32)
    for slot in range(slots):
        held = jnp.broadcast_to(column[:, slot:slot + 1], (band, 128))
        codes = jnp.where((held == wanted) & (held >= 0), slot, codes)
    inv[...] = jnp.full(inv.shape, -1, jnp.int32)
    inv[:band, :] = codes
    put_v[...] = jnp.where(column >= 0, (column - base) >> 1, -1)
    pl.semaphore_wait(barrier, 2 + has_to.astype(jnp.int32) + has_from.astype(jnp.int32))

    def remote(src, dst, send, recv, device):
        return pltpu.make_async_remote_copy(
            src_ref=src, dst_ref=dst, send_sem=send, recv_sem=recv,
            device_id=device, device_id_type=MESH,
        )

    def x_copy(row):
        return remote(vals.at[row, 0], x_buf.at[row], x_send.at[row], x_recv.at[row], x_id)

    def f_copy(row):
        return remote(x_buf.at[row], f_buf.at[row], f_send.at[row], f_recv.at[row], to_id)

    def sent_row(h):
        return jnp.where(odd == 1, band - 1 - h, h)

    def got_row(h):
        return jnp.where(odd == 1, h, band - 1 - h)

    def got_chunk(m):
        return jnp.where(odd == 1, m, chunks - 1 - m)

    tab_c = remote(inv, inv_o, t_send.at[0], t_recv.at[0], core_id)
    tab_x = remote(inv, inv_x, t_send.at[1], t_recv.at[1], x_id)
    tab_f = remote(inv_x, inv_f, t_send.at[2], t_recv.at[2], to_id)
    core = remote(vals.at[:, 0], both.at[p], c_sem.at[0], c_sem.at[1], core_id)
    tab_x.start()
    tab_c.start()
    x_copy(sent_row(0)).start()
    core.start()
    for h in range(1, band):
        x_copy(sent_row(h)).start()

    acc[...] = jnp.zeros_like(acc)
    own.wait()
    tab_x.wait()

    @pl.when(has_to)
    def _():
        tab_f.start()

    core.wait()
    tab_c.wait()

    def a_row(i, carry):
        at = pl.ds(pl.multiple_of(i * 64, 64), 64)
        low = low_half((8, 8, 128))
        held = []
        for u in range(slots // 2):
            even = both[0, i, :, u * 128:(u + 1) * 128].reshape(8, 8, 128)
            odd = both[1, i, :, u * 128:(u + 1) * 128].reshape(8, 8, 128)
            held.append((jnp.where(low, even, odd), rolled(jnp.where(low, odd, even))))
        mine, other = inv[pl.ds(i, 1), :], inv_o[pl.ds(i, 1), :]
        first = jnp.where(p == 0, mine, other)
        second = jnp.where(p == 0, other, mine)
        for t in range(k_tiles):
            hi, lo = split(picked(pair(first, OWN_AT + t, second, OWN_AT + t), held))
            a_hi[t, at, :] = hi
            a_lo[t, at, :] = lo
        return carry

    lax.fori_loop(0, band, a_row, 0)

    def spread(chunk, table, first, load):
        for r in range(CHUNK):
            stage[r] = load(chunk * CHUNK + r)
            codes = table[pl.ds(chunk * CHUNK + r, 1), :]
            held = []
            for u in range(slots // 2):
                tile = stage[r, :, u * 128:(u + 1) * 128].reshape(8, 8, 128)
                held.append((tile, rolled(tile)))
            for t in range(tiles):
                at = first + 2 * t
                hi, lo = split(picked(pair(codes, at, codes, at + 1), held))
                b_hi[r * 64:(r + 1) * 64, t * 128:(t + 1) * 128] = hi
                b_lo[r * 64:(r + 1) * 64, t * 128:(t + 1) * 128] = lo

    def multiply(k_tile, at):
        left_hi = a_hi[k_tile, at, :]
        left = jnp.concatenate([left_hi, left_hi, a_lo[k_tile, at, :]], axis=1)
        for t in range(0, tiles, 2):
            wide = slice(t * 128, (t + 2) * 128)
            right_hi = b_hi[:, wide]
            right = jnp.concatenate([right_hi, b_lo[:, wide], right_hi], axis=0)
            part = jnp.dot(left, right, preferred_element_type=jnp.float32)
            acc[t, at, :] += part[:, :128]
            acc[t + 1, at, :] += part[:, 128:]

    own_tile = REACH // 2
    everything = pl.ds(0, band * 64)

    def forward(h):
        row = got_row(h)
        x_copy(row).wait_recv()

        @pl.when(has_to)
        def _():
            f_copy(row).start()

    def from_relay(row):
        f_copy(row).wait_recv()
        return f_buf[row]

    def relay_chunk(m):
        spread(got_chunk(m), inv_f, F_AT, from_relay)
        return own_tile - x_shift + got_chunk(m)

    def step(m, carry):
        forward(CHUNK * m)
        spread(m, inv, OWN_AT, lambda row: both[p, row])
        multiply(own_tile + m, everything)
        for r in range(1, CHUNK):
            forward(CHUNK * m + r)
        spread(got_chunk(m), inv_x, X_AT, lambda row: x_buf[row])
        multiply(own_tile + x_shift + got_chunk(m), everything)

        @pl.when(has_from & (m >= 1))
        def _():
            @pl.when(m == 1)
            def _():
                tab_f.wait_recv()

            multiply(relay_chunk(m - 1), everything)

        return carry

    lax.fori_loop(0, chunks, step, 0)

    def out_row(i, carry):
        at = pl.ds(pl.multiple_of(i * 64, 64), 64)
        held = []
        for u in range(tiles):
            tile = acc[u, at, :].reshape(8, 8, 128)
            held.append((tile, rolled(tile)))
        codes = put_v[pl.ds(i, 1), :]
        for t in range(slots // 2):
            put = 2 * t
            x = picked(pair(codes, put, codes, put + 1), held)
            out[i, 0, :, t * 128:(t + 1) * 128] = x.reshape(64, 128)
        return carry

    last = got_chunk(chunks - 1) * CHUNK
    start = jnp.where(odd == 1, 0, CHUNK)
    lax.fori_loop(start, start + band - CHUNK, out_row, 0)

    @pl.when(has_from)
    def _():
        k_tile = relay_chunk(chunks - 1)
        multiply(k_tile, pl.ds(pl.multiple_of(last * 64, 128), CHUNK * 64))

    lax.fori_loop(last, last + CHUNK, out_row, 0)

    for row in range(band):
        x_copy(row).wait_send()

    @pl.when(has_to)
    def _():
        tab_f.wait_send()
        for row in range(band):
            f_copy(row).wait_send()


def local(n_col, block_values, block_cols):
    band, _, side, _ = block_values.shape
    slots = block_cols.shape[2]
    rows = -(-band // 8) * 8
    k_tiles = (2 * REACH + band) // 2
    tiles = (k_tiles + 1) // 2
    dma = pltpu.SemaphoreType.DMA
    return pl.pallas_call(
        functools.partial(kernel, n_col, band, slots),
        out_shape=jax.ShapeDtypeStruct(block_values.shape, jnp.float32),
        in_specs=[
            pl.BlockSpec(memory_space=pltpu.HBM),
            pl.BlockSpec(memory_space=pltpu.HBM),
        ],
        out_specs=pl.BlockSpec(memory_space=pltpu.VMEM),
        scratch_shapes=[
            pltpu.VMEM((2, band, side, slots * side), jnp.float32),
            pltpu.VMEM((band, side, slots * side), jnp.float32),
            pltpu.VMEM((band, side, slots * side), jnp.float32),
            pltpu.VMEM((CHUNK, side, slots * side), jnp.float32),
            pltpu.VMEM((CHUNK * side, tiles * 128), jnp.bfloat16),
            pltpu.VMEM((CHUNK * side, tiles * 128), jnp.bfloat16),
            pltpu.VMEM((k_tiles, band * side, 128), jnp.bfloat16),
            pltpu.VMEM((k_tiles, band * side, 128), jnp.bfloat16),
            pltpu.VMEM((tiles, band * side, 128), jnp.float32),
            pltpu.VMEM(block_cols.shape, jnp.int32),
            pltpu.VMEM((band, slots), jnp.int32),
            pltpu.VMEM((rows, 128), jnp.int32),
            pltpu.VMEM((rows, 128), jnp.int32),
            pltpu.VMEM((rows, 128), jnp.int32),
            pltpu.VMEM((rows, 128), jnp.int32),
            dma((band,)), dma((band,)), dma((band,)), dma((band,)),
            dma((2,)), dma((3,)), dma((3,)), dma((2,)),
        ],
        compiler_params=pltpu.CompilerParams(
            collective_id=0, has_side_effects=True, vmem_limit_bytes=48 * 1024 * 1024
        ),
    )(block_values, block_cols)


def solution(mesh):
    in_specs = (P(("groups", "col"), "row", None, None), P(("groups", "col"), "row", None))
    out_specs = P(("groups", "col"), "row", None, None)
    return jax.shard_map(
        functools.partial(local, mesh.shape["col"]),
        mesh=mesh, in_specs=in_specs, out_specs=out_specs, check_vma=False,
    )
```

```python
import functools

import jax
import jax.numpy as jnp
from jax import lax
from jax.experimental import pallas as pl
from jax.experimental.pallas import tpu as pltpu
from jax.sharding import PartitionSpec as P

REACH = 10
CHUNK = 2
PIECE = 32
PARTS = 2
OWN_AT, X_AT, F_AT = 0, 32, 64
MESH = pl.DeviceIdType.MESH


def picked(codes, tiles):
    high = (lax.broadcasted_iota(jnp.int32, (8, 128), 1) >= 64).astype(jnp.int32)
    kept, turned = codes - high, codes + high
    x = jnp.zeros((8, 8, 128), jnp.float32)
    for u, (plain, rolled) in enumerate(tiles):
        x = jnp.where((kept == 2 * u)[None], plain, x)
        x = jnp.where((turned == 2 * u + 1)[None], rolled, x)
    return x


def rolled(x):
    return pltpu.roll(x.reshape(64, 128), 64, 1).reshape(8, 8, 128)


def low_half(shape):
    return lax.broadcasted_iota(jnp.int32, shape, len(shape) - 1) < 64


def pair(low, low_at, high, high_at):
    first = jnp.broadcast_to(low[:, low_at:low_at + 1], (8, 128))
    second = jnp.broadcast_to(high[:, high_at:high_at + 1], (8, 128))
    return jnp.where(low_half((8, 128)), first, second)


def split(x):
    x = x.reshape(64, 128)
    hi = x.astype(jnp.bfloat16)
    return hi, (x - hi.astype(jnp.float32)).astype(jnp.bfloat16)


def kernel(
    n_col, band, slots, vals, cols, out,
    both, x_buf, f_buf, out_v, stage, b_hi, b_lo, a_hi, a_lo, acc, cols_v, put_v, inv, inv_o, inv_x, inv_f,
    x_send, x_recv, f_send, f_recv, c_sem, t_send, t_recv, l_sem,
):
    g, p, c = lax.axis_index("groups"), lax.axis_index("row"), lax.axis_index("col")
    chunks = band // CHUNK
    tiles = acc.shape[0]
    k_tiles = a_hi.shape[0]
    half = band // 2
    odd = lax.rem(c, 2)
    x_peer = c + 1 - 2 * odd
    x_shift = half * (1 - 2 * odd)
    f_to, f_from = c + 2 - 4 * odd, c - 2 + 4 * odd
    has_to = (f_to >= 0) & (f_to < n_col)
    has_from = (f_from >= 0) & (f_from < n_col)
    core_id, x_id = (g, 1 - p, c), (g, p, x_peer)
    to_id = (g, p, jnp.clip(f_to, 0, n_col - 1))
    from_id = (g, p, jnp.clip(f_from, 0, n_col - 1))

    own = pltpu.make_async_copy(vals.at[:, 0], both.at[p], l_sem.at[0])
    lists = pltpu.make_async_copy(cols, cols_v, l_sem.at[1])
    lists.start()
    own.start()

    barrier = pltpu.get_barrier_semaphore()
    for peer in (core_id, x_id):
        pl.semaphore_signal(barrier, inc=1, device_id=peer, device_id_type=MESH)

    @pl.when(has_to)
    def _():
        pl.semaphore_signal(barrier, inc=1, device_id=to_id, device_id_type=MESH)

    @pl.when(has_from)
    def _():
        pl.semaphore_signal(barrier, inc=1, device_id=from_id, device_id_type=MESH)

    lists.wait()
    column = cols_v[:, 0, :]
    base = c * band - REACH + p
    lane = lax.broadcasted_iota(jnp.int32, (band, 128), 1)
    view = lane >> 5
    moved = jnp.where(view == 1, x_shift, jnp.where(view == 2, -x_shift, 0))
    wanted = base + 2 * ((lane & 31) + moved)
    codes = jnp.full((band, 128), -1, jnp.int32)
    for slot in range(slots):
        held = jnp.broadcast_to(column[:, slot:slot + 1], (band, 128))
        codes = jnp.where((held == wanted) & (held >= 0), slot, codes)
    inv[...] = jnp.full(inv.shape, -1, jnp.int32)
    inv[:band, :] = codes
    put_v[...] = jnp.where(column >= 0, (column - base) >> 1, -1)
    pl.semaphore_wait(barrier, 2 + has_to.astype(jnp.int32) + has_from.astype(jnp.int32))

    def remote(src, dst, send, recv, device):
        return pltpu.make_async_remote_copy(
            src_ref=src, dst_ref=dst, send_sem=send, recv_sem=recv,
            device_id=device, device_id_type=MESH,
        )

    def x_copy(row, part):
        at, sem = pl.ds(part * PIECE, PIECE), row * PARTS + part
        return remote(
            vals.at[row, 0, at], x_buf.at[row, at], x_send.at[sem], x_recv.at[sem], x_id
        )

    def f_copy(row, part):
        at, sem = pl.ds(part * PIECE, PIECE), row * PARTS + part
        return remote(
            x_buf.at[row, at], f_buf.at[row, at], f_send.at[sem], f_recv.at[sem], to_id
        )

    def sent_row(h):
        return jnp.where(odd == 1, band - 1 - h, h)

    def got_row(h):
        return jnp.where(odd == 1, h, band - 1 - h)

    def got_chunk(m):
        return jnp.where(odd == 1, m, chunks - 1 - m)

    tab_c = remote(inv, inv_o, t_send.at[0], t_recv.at[0], core_id)
    tab_x = remote(inv, inv_x, t_send.at[1], t_recv.at[1], x_id)
    tab_f = remote(inv_x, inv_f, t_send.at[2], t_recv.at[2], to_id)
    core = remote(vals.at[:, 0], both.at[p], c_sem.at[0], c_sem.at[1], core_id)
    tab_x.start()
    tab_c.start()
    x_copy(sent_row(0), 0).start()
    core.start()
    for h in range(1, band * PARTS):
        x_copy(sent_row(h // PARTS), h % PARTS).start()

    acc[...] = jnp.zeros_like(acc)
    own.wait()
    tab_x.wait()

    @pl.when(has_to)
    def _():
        tab_f.start()

    def a_row(i, carry):
        at = pl.ds(pl.multiple_of(i * 64, 64), 64)
        low = low_half((8, 8, 128))
        held = []
        for u in range(slots // 2):
            even = both[0, i, :, u * 128:(u + 1) * 128].reshape(8, 8, 128)
            odd = both[1, i, :, u * 128:(u + 1) * 128].reshape(8, 8, 128)
            held.append((jnp.where(low, even, odd), rolled(jnp.where(low, odd, even))))
        mine, other = inv[pl.ds(i, 1), :], inv_o[pl.ds(i, 1), :]
        first = jnp.where(p == 0, mine, other)
        second = jnp.where(p == 0, other, mine)
        for t in range(k_tiles):
            hi, lo = split(picked(pair(first, OWN_AT + t, second, OWN_AT + t), held))
            a_hi[t, at, :] = hi
            a_lo[t, at, :] = lo
        return carry

    def spread(chunk, table, first, load):
        for r in range(CHUNK):
            stage[r] = load(chunk * CHUNK + r)
            codes = table[pl.ds(chunk * CHUNK + r, 1), :]
            held = []
            for u in range(slots // 2):
                tile = stage[r, :, u * 128:(u + 1) * 128].reshape(8, 8, 128)
                held.append((tile, rolled(tile)))
            for t in range(tiles):
                at = first + 2 * t
                hi, lo = split(picked(pair(codes, at, codes, at + 1), held))
                b_hi[r * 64:(r + 1) * 64, t * 128:(t + 1) * 128] = hi
                b_lo[r * 64:(r + 1) * 64, t * 128:(t + 1) * 128] = lo

    def multiply(k_tile, at):
        left_hi = a_hi[k_tile, at, :]
        left = jnp.concatenate([left_hi, left_hi, a_lo[k_tile, at, :]], axis=1)
        for t in range(0, tiles, 2):
            wide = slice(t * 128, (t + 2) * 128)
            right_hi = b_hi[:, wide]
            right = jnp.concatenate([right_hi, b_lo[:, wide], right_hi], axis=0)
            part = jnp.dot(left, right, preferred_element_type=jnp.float32)
            acc[t, at, :] += part[:, :128]
            acc[t + 1, at, :] += part[:, 128:]

    own_tile = REACH // 2
    everything = pl.ds(0, band * 64)

    def forward(h):
        row, part = got_row(h // PARTS), lax.rem(h, PARTS)
        x_copy(row, part).wait_recv()

        @pl.when(has_to)
        def _():
            f_copy(row, part).start()

    def from_relay(row):
        for part in range(PARTS):
            f_copy(row, part).wait_recv()
        return f_buf[row]

    def relay_chunk(m):
        spread(got_chunk(m), inv_f, F_AT, from_relay)
        return own_tile - x_shift + got_chunk(m)

    def step(m, carry):
        h = CHUNK * PARTS * m

        @pl.when(m == 0)
        def _():
            core.wait()
            tab_c.wait()
            lax.fori_loop(0, half, a_row, 0)

        forward(h + 1)

        @pl.when(m == 0)
        def _():
            lax.fori_loop(half, band, a_row, 0)

        spread(m, inv, OWN_AT, lambda row: both[p, row])
        forward(h + 2)
        multiply(own_tile + m, everything)

        @pl.when(has_from & (m >= 1))
        def _():
            @pl.when(m == 1)
            def _():
                tab_f.wait_recv()

            multiply(relay_chunk(m - 1), everything)

        for later in range(3, CHUNK * PARTS):
            forward(h + later)
        spread(got_chunk(m), inv_x, X_AT, lambda row: x_buf[row])

        @pl.when(m < chunks - 1)
        def _():
            forward(h + CHUNK * PARTS)

        multiply(own_tile + x_shift + got_chunk(m), everything)
        return carry

    forward(0)
    lax.fori_loop(0, chunks, step, 0)

    def out_row(i, carry):
        at = pl.ds(pl.multiple_of(i * 64, 64), 64)
        held = []
        for u in range(tiles):
            tile = acc[u, at, :].reshape(8, 8, 128)
            held.append((tile, rolled(tile)))
        codes = put_v[pl.ds(i, 1), :]
        for t in range(slots // 2):
            put = 2 * t
            x = picked(pair(codes, put, codes, put + 1), held)
            out_v[i, :, t * 128:(t + 1) * 128] = x.reshape(64, 128)
        return carry

    last = got_chunk(chunks - 1) * CHUNK
    start = jnp.where(odd == 1, 0, CHUNK)
    lax.fori_loop(start, start + band - CHUNK, out_row, 0)
    early, late = pl.ds(start, band - CHUNK), pl.ds(last, CHUNK)
    write_early = pltpu.make_async_copy(out_v.at[early], out.at[early, 0], l_sem.at[2])
    write_late = pltpu.make_async_copy(out_v.at[late], out.at[late, 0], l_sem.at[3])
    write_early.start()

    @pl.when(has_from)
    def _():
        k_tile = relay_chunk(chunks - 1)
        multiply(k_tile, pl.ds(pl.multiple_of(last * 64, 128), CHUNK * 64))

    lax.fori_loop(last, last + CHUNK, out_row, 0)
    write_late.start()

    for row in range(band):
        for part in range(PARTS):
            x_copy(row, part).wait_send()

    @pl.when(has_to)
    def _():
        tab_f.wait_send()
        for row in range(band):
            for part in range(PARTS):
                f_copy(row, part).wait_send()

    write_early.wait()
    write_late.wait()


def local(n_col, block_values, block_cols):
    band, _, side, _ = block_values.shape
    slots = block_cols.shape[2]
    rows = -(-band // 8) * 8
    k_tiles = (2 * REACH + band) // 2
    tiles = (k_tiles + 1) // 2
    pieces = band * PARTS
    dma = pltpu.SemaphoreType.DMA
    return pl.pallas_call(
        functools.partial(kernel, n_col, band, slots),
        out_shape=jax.ShapeDtypeStruct(block_values.shape, jnp.float32),
        in_specs=[
            pl.BlockSpec(memory_space=pltpu.HBM),
            pl.BlockSpec(memory_space=pltpu.HBM),
        ],
        out_specs=pl.BlockSpec(memory_space=pltpu.HBM),
        scratch_shapes=[
            pltpu.VMEM((2, band, side, slots * side), jnp.float32),
            pltpu.VMEM((band, side, slots * side), jnp.float32),
            pltpu.VMEM((band, side, slots * side), jnp.float32),
            pltpu.VMEM((band, side, slots * side), jnp.float32),
            pltpu.VMEM((CHUNK, side, slots * side), jnp.float32),
            pltpu.VMEM((CHUNK * side, tiles * 128), jnp.bfloat16),
            pltpu.VMEM((CHUNK * side, tiles * 128), jnp.bfloat16),
            pltpu.VMEM((k_tiles, band * side, 128), jnp.bfloat16),
            pltpu.VMEM((k_tiles, band * side, 128), jnp.bfloat16),
            pltpu.VMEM((tiles, band * side, 128), jnp.float32),
            pltpu.VMEM(block_cols.shape, jnp.int32),
            pltpu.VMEM((band, slots), jnp.int32),
            pltpu.VMEM((rows, 128), jnp.int32),
            pltpu.VMEM((rows, 128), jnp.int32),
            pltpu.VMEM((rows, 128), jnp.int32),
            pltpu.VMEM((rows, 128), jnp.int32),
            dma((pieces,)), dma((pieces,)), dma((pieces,)), dma((pieces,)),
            dma((2,)), dma((3,)), dma((3,)), dma((4,)),
        ],
        compiler_params=pltpu.CompilerParams(
            collective_id=0, has_side_effects=True, vmem_limit_bytes=60 * 1024 * 1024
        ),
    )(block_values, block_cols)


def solution(mesh):
    in_specs = (P(("groups", "col"), "row", None, None), P(("groups", "col"), "row", None))
    out_specs = P(("groups", "col"), "row", None, None)
    return jax.shard_map(
        functools.partial(local, mesh.shape["col"]),
        mesh=mesh, in_specs=in_specs, out_specs=out_specs, check_vma=False,
    )
```

```python
import functools

import jax
import jax.numpy as jnp
from jax import lax
from jax.experimental import pallas as pl
from jax.experimental.pallas import tpu as pltpu
from jax.sharding import PartitionSpec as P

REACH = 10
CHUNK = 2
PIECE = 32
PARTS = 2
OWN_AT, X_AT, F_AT = 0, 32, 64
MESH = pl.DeviceIdType.MESH


def picked(codes, tiles):
    high = (lax.broadcasted_iota(jnp.int32, (8, 128), 1) >= 64).astype(jnp.int32)
    kept, turned = codes - high, codes + high
    x = jnp.zeros((8, 8, 128), jnp.float32)
    for u, (plain, rolled) in enumerate(tiles):
        x = jnp.where((kept == 2 * u)[None], plain, x)
        x = jnp.where((turned == 2 * u + 1)[None], rolled, x)
    return x


def rolled(x):
    return pltpu.roll(x.reshape(64, 128), 64, 1).reshape(8, 8, 128)


def low_half(shape):
    return lax.broadcasted_iota(jnp.int32, shape, len(shape) - 1) < 64


def pair(low, low_at, high, high_at):
    first = jnp.broadcast_to(low[:, low_at:low_at + 1], (8, 128))
    second = jnp.broadcast_to(high[:, high_at:high_at + 1], (8, 128))
    return jnp.where(low_half((8, 128)), first, second)


def split(x):
    x = x.reshape(64, 128)
    hi = x.astype(jnp.bfloat16)
    return hi, (x - hi.astype(jnp.float32)).astype(jnp.bfloat16)


def kernel(
    n_col, band, slots, vals, cols, out,
    both, x_buf, f_buf, stage, b_hi, b_lo, a_hi, a_lo, acc, cols_v, put_v, inv, inv_o, inv_x, inv_f,
    x_send, x_recv, f_send, f_recv, c_sem, t_send, t_recv, l_sem,
):
    g, p, c = lax.axis_index("groups"), lax.axis_index("row"), lax.axis_index("col")
    chunks = band // CHUNK
    tiles = acc.shape[0]
    k_tiles = a_hi.shape[0]
    half = band // 2
    odd = lax.rem(c, 2)
    x_peer = c + 1 - 2 * odd
    x_shift = half * (1 - 2 * odd)
    f_to, f_from = c + 2 - 4 * odd, c - 2 + 4 * odd
    has_to = (f_to >= 0) & (f_to < n_col)
    has_from = (f_from >= 0) & (f_from < n_col)
    core_id, x_id = (g, 1 - p, c), (g, p, x_peer)
    to_id = (g, p, jnp.clip(f_to, 0, n_col - 1))
    from_id = (g, p, jnp.clip(f_from, 0, n_col - 1))

    own = pltpu.make_async_copy(vals.at[:, 0], both.at[p], l_sem.at[0])
    lists = pltpu.make_async_copy(cols, cols_v, l_sem.at[1])
    lists.start()
    own.start()

    barrier = pltpu.get_barrier_semaphore()
    for peer in (core_id, x_id):
        pl.semaphore_signal(barrier, inc=1, device_id=peer, device_id_type=MESH)

    @pl.when(has_to)
    def _():
        pl.semaphore_signal(barrier, inc=1, device_id=to_id, device_id_type=MESH)

    @pl.when(has_from)
    def _():
        pl.semaphore_signal(barrier, inc=1, device_id=from_id, device_id_type=MESH)

    pl.semaphore_wait(barrier, 2 + has_to.astype(jnp.int32) + has_from.astype(jnp.int32))

    def remote(src, dst, send, recv, device):
        return pltpu.make_async_remote_copy(
            src_ref=src, dst_ref=dst, send_sem=send, recv_sem=recv,
            device_id=device, device_id_type=MESH,
        )

    def x_copy(row, part):
        at, sem = pl.ds(part * PIECE, PIECE), row * PARTS + part
        return remote(
            vals.at[row, 0, at], x_buf.at[row, at], x_send.at[sem], x_recv.at[sem], x_id
        )

    def f_copy(row, part):
        at, sem = pl.ds(part * PIECE, PIECE), row * PARTS + part
        return remote(
            x_buf.at[row, at], f_buf.at[row, at], f_send.at[sem], f_recv.at[sem], to_id
        )

    def sent_row(h):
        return jnp.where(odd == 1, band - 1 - h, h)

    def got_row(h):
        return jnp.where(odd == 1, h, band - 1 - h)

    def got_chunk(m):
        return jnp.where(odd == 1, m, chunks - 1 - m)

    tab_c = remote(inv, inv_o, t_send.at[0], t_recv.at[0], core_id)
    tab_x = remote(inv, inv_x, t_send.at[1], t_recv.at[1], x_id)
    tab_f = remote(inv_x, inv_f, t_send.at[2], t_recv.at[2], to_id)
    core = remote(vals.at[:, 0], both.at[p], c_sem.at[0], c_sem.at[1], core_id)
    x_copy(sent_row(0), 0).start()
    core.start()

    lists.wait()
    column = cols_v[:, 0, :]
    base = c * band - REACH + p
    lane = lax.broadcasted_iota(jnp.int32, (band, 128), 1)
    view = lane >> 5
    moved = jnp.where(view == 1, x_shift, jnp.where(view == 2, -x_shift, 0))
    wanted = base + 2 * ((lane & 31) + moved)
    codes = jnp.full((band, 128), -1, jnp.int32)
    for slot in range(slots):
        held = jnp.broadcast_to(column[:, slot:slot + 1], (band, 128))
        codes = jnp.where((held == wanted) & (held >= 0), slot, codes)
    inv[...] = jnp.full(inv.shape, -1, jnp.int32)
    inv[:band, :] = codes
    put_v[...] = jnp.where(column >= 0, (column - base) >> 1, -1)
    tab_x.start()
    tab_c.start()
    for h in range(1, band * PARTS):
        x_copy(sent_row(h // PARTS), h % PARTS).start()

    acc[...] = jnp.zeros_like(acc)
    own.wait()
    tab_x.wait()

    @pl.when(has_to)
    def _():
        tab_f.start()

    def a_row(i, carry):
        at = pl.ds(pl.multiple_of(i * 64, 64), 64)
        low = low_half((8, 8, 128))
        held = []
        for u in range(slots // 2):
            even = both[0, i, :, u * 128:(u + 1) * 128].reshape(8, 8, 128)
            odd = both[1, i, :, u * 128:(u + 1) * 128].reshape(8, 8, 128)
            held.append((jnp.where(low, even, odd), rolled(jnp.where(low, odd, even))))
        mine, other = inv[pl.ds(i, 1), :], inv_o[pl.ds(i, 1), :]
        first = jnp.where(p == 0, mine, other)
        second = jnp.where(p == 0, other, mine)
        for t in range(k_tiles):
            hi, lo = split(picked(pair(first, OWN_AT + t, second, OWN_AT + t), held))
            a_hi[t, at, :] = hi
            a_lo[t, at, :] = lo
        return carry

    def spread(chunk, table, first, load):
        for r in range(CHUNK):
            row = jnp.where(odd == 1, r, CHUNK - 1 - r)
            at_row = pl.ds(pl.multiple_of(row * 64, 64), 64)
            stage[r] = load(chunk * CHUNK + row)
            codes = table[pl.ds(chunk * CHUNK + row, 1), :]
            held = []
            for u in range(slots // 2):
                tile = stage[r, :, u * 128:(u + 1) * 128].reshape(8, 8, 128)
                held.append((tile, rolled(tile)))
            for t in range(tiles):
                at = first + 2 * t
                hi, lo = split(picked(pair(codes, at, codes, at + 1), held))
                b_hi[at_row, t * 128:(t + 1) * 128] = hi
                b_lo[at_row, t * 128:(t + 1) * 128] = lo

    def multiply(k_tile, at):
        left_hi = a_hi[k_tile, at, :]
        left = jnp.concatenate([left_hi, left_hi, a_lo[k_tile, at, :]], axis=1)
        for t in range(0, tiles, 2):
            wide = slice(t * 128, (t + 2) * 128)
            right_hi = b_hi[:, wide]
            right = jnp.concatenate([right_hi, b_lo[:, wide], right_hi], axis=0)
            part = jnp.dot(left, right, preferred_element_type=jnp.float32)
            acc[t, at, :] += part[:, :128]
            acc[t + 1, at, :] += part[:, 128:]

    own_tile = REACH // 2
    everything = pl.ds(0, band * 64)

    def forward(h):
        row, part = got_row(h // PARTS), lax.rem(h, PARTS)
        x_copy(row, part).wait_recv()

        @pl.when(has_to)
        def _():
            f_copy(row, part).start()

    def from_relay(row):
        for part in range(PARTS):
            f_copy(row, part).wait_recv()
        return f_buf[row]

    def relay_chunk(m):
        spread(got_chunk(m), inv_f, F_AT, from_relay)
        return own_tile - x_shift + got_chunk(m)

    def step(m, carry):
        h = CHUNK * PARTS * m

        @pl.when(m == 0)
        def _():
            core.wait()
            tab_c.wait()
            lax.fori_loop(0, half, a_row, 0)

        forward(h + 1)

        @pl.when(m == 0)
        def _():
            lax.fori_loop(half, band, a_row, 0)

        spread(m, inv, OWN_AT, lambda row: both[p, row])
        forward(h + 2)
        multiply(own_tile + m, everything)

        @pl.when(has_from & (m >= 1))
        def _():
            @pl.when(m == 1)
            def _():
                tab_f.wait_recv()

            multiply(relay_chunk(m - 1), everything)

        for later in range(3, CHUNK * PARTS):
            forward(h + later)
        spread(got_chunk(m), inv_x, X_AT, lambda row: x_buf[row])

        @pl.when(m < chunks - 1)
        def _():
            forward(h + CHUNK * PARTS)

        multiply(own_tile + x_shift + got_chunk(m), everything)
        return carry

    forward(0)
    lax.fori_loop(0, chunks, step, 0)

    def out_row(i, carry):
        at = pl.ds(pl.multiple_of(i * 64, 64), 64)
        held = []
        for u in range(tiles):
            tile = acc[u, at, :].reshape(8, 8, 128)
            held.append((tile, rolled(tile)))
        codes = put_v[pl.ds(i, 1), :]
        for t in range(slots // 2):
            put = 2 * t
            x = picked(pair(codes, put, codes, put + 1), held)
            out[i, 0, :, t * 128:(t + 1) * 128] = x.reshape(64, 128)
        return carry

    last = got_chunk(chunks - 1) * CHUNK
    start = jnp.where(odd == 1, 0, CHUNK)
    lax.fori_loop(start, start + band - CHUNK, out_row, 0)

    @pl.when(has_from)
    def _():
        k_tile = relay_chunk(chunks - 1)
        multiply(k_tile, pl.ds(pl.multiple_of(last * 64, 128), CHUNK * 64))

    lax.fori_loop(last, last + CHUNK, out_row, 0)

    for row in range(band):
        for part in range(PARTS):
            x_copy(row, part).wait_send()

    @pl.when(has_to)
    def _():
        tab_f.wait_send()
        for row in range(band):
            for part in range(PARTS):
                f_copy(row, part).wait_send()


def local(n_col, block_values, block_cols):
    band, _, side, _ = block_values.shape
    slots = block_cols.shape[2]
    rows = -(-band // 8) * 8
    k_tiles = (2 * REACH + band) // 2
    tiles = (k_tiles + 1) // 2
    pieces = band * PARTS
    dma = pltpu.SemaphoreType.DMA
    return pl.pallas_call(
        functools.partial(kernel, n_col, band, slots),
        out_shape=jax.ShapeDtypeStruct(block_values.shape, jnp.float32),
        in_specs=[
            pl.BlockSpec(memory_space=pltpu.HBM),
            pl.BlockSpec(memory_space=pltpu.HBM),
        ],
        out_specs=pl.BlockSpec(memory_space=pltpu.VMEM),
        scratch_shapes=[
            pltpu.VMEM((2, band, side, slots * side), jnp.float32),
            pltpu.VMEM((band, side, slots * side), jnp.float32),
            pltpu.VMEM((band, side, slots * side), jnp.float32),
            pltpu.VMEM((CHUNK, side, slots * side), jnp.float32),
            pltpu.VMEM((CHUNK * side, tiles * 128), jnp.bfloat16),
            pltpu.VMEM((CHUNK * side, tiles * 128), jnp.bfloat16),
            pltpu.VMEM((k_tiles, band * side, 128), jnp.bfloat16),
            pltpu.VMEM((k_tiles, band * side, 128), jnp.bfloat16),
            pltpu.VMEM((tiles, band * side, 128), jnp.float32),
            pltpu.VMEM(block_cols.shape, jnp.int32),
            pltpu.VMEM((band, slots), jnp.int32),
            pltpu.VMEM((rows, 128), jnp.int32),
            pltpu.VMEM((rows, 128), jnp.int32),
            pltpu.VMEM((rows, 128), jnp.int32),
            pltpu.VMEM((rows, 128), jnp.int32),
            dma((pieces,)), dma((pieces,)), dma((pieces,)), dma((pieces,)),
            dma((2,)), dma((3,)), dma((3,)), dma((2,)),
        ],
        compiler_params=pltpu.CompilerParams(
            collective_id=0, has_side_effects=True, vmem_limit_bytes=48 * 1024 * 1024
        ),
    )(block_values, block_cols)


def solution(mesh):
    in_specs = (P(("groups", "col"), "row", None, None), P(("groups", "col"), "row", None))
    out_specs = P(("groups", "col"), "row", None, None)
    return jax.shard_map(
        functools.partial(local, mesh.shape["col"]),
        mesh=mesh, in_specs=in_specs, out_specs=out_specs, check_vma=False,
    )
```
